1024 devices in a mesh: rep: 128 (over y_lo, z, core), fsdp: 8 (over x, y_hi).
Axes of the slice: x: 4, y: 4 (y_hi: 2, y_lo: 2; y = y_hi * 2 + y_lo), z: 32, core: 2. Of those that a mesh axis runs over, the one named last changes fastest.
Arguments:
- tokens: bfloat16 [229376, 6144], P(('rep', 'fsdp')), may hold values from -6 to 6
- query_weight: bfloat16 [128, 6144, 128], P('rep', 'fsdp'), may hold values from -0.078125 to 0.078125
- global_params: float32 [6144, 256], P('fsdp'), may hold values from -6 to 6
- local_params: bfloat16 [128, 6144, 256], P('rep', 'fsdp'), may hold values from -24 to 24
- momentum: float32 [8, 6144, 256], P(None, ('fsdp', 'rep')), may hold values from -0.6 to 0.6
- inner_steps: int32 [128], replicated, may hold values from 20 to 100
- replica_tokens: int32 [128], replicated, may hold values from 100000 to 400000
- plan: int32 [1], replicated, may hold values from 0 to 7
Outputs:
- queries: bfloat16 [229376, 128], P(('rep', 'fsdp'))
- new_params: float32 [6144, 256], P('fsdp')
- new_momentum: float32 [6144, 256], P(('fsdp', 'rep'))
The draws below stay inside these ranges and needn't reach their ends.
All inputs are finite; a program needn't handle non-finite values. Where the reference program divides by a largest or mean magnitude, that divisor is 1e-20 or more.
Results may differ from the reference program's by a relative error of at most 0.0028.
Values may be sent and summed in bfloat16 or wider, within the bound.
A program may use at most 32 MiB of HBM per device.

```python
import math
import jax
import jax.numpy as jnp
from jax import lax

D = 6144
HD = 128
BLOCK = 128
FRAGS = 8
C = 256
REPS = 128
TOKENS = 229376


def with_ends(drawn, stream_key, low, high):
    longest = drawn.shape.index(max(drawn.shape))
    spots = []
    for shift in (0, 1):
        where = [jax.random.randint(jax.random.fold_in(stream_key, axis), (), 0, length) for axis, length in enumerate(drawn.shape)]
        where[longest] = (where[longest] + shift) % drawn.shape[longest]
        spots.append(tuple(where))
    return drawn.at[spots[0]].set(low).at[spots[1]].set(high)


def with_spikes(result, key, source, target, parts, factor):
    owner, partner = [(jnp.arange(result.shape[dim]) // (result.shape[dim] // parts)).reshape([-1 if axis == dim else 1 for axis in range(result.ndim)]) for dim in (source, target)]
    chosen = jax.random.permutation(key, parts)[partner]
    strong = (owner == chosen) | (owner == (partner + parts // 2) % parts)
    return jnp.where(strong, factor * result, result)


def levels(rng, extent, shards, smallest, high):
    def one(dim, shards_of):
        heights = jax.random.uniform(jax.random.fold_in(jax.random.fold_in(rng, 6), dim), (shards_of,), jnp.float32, smallest / len(shards), high / len(shards))
        return jnp.repeat(jnp.exp(heights), extent[dim] // shards_of).reshape((-1,) + (1,) * (len(extent) - dim - 1))

    loudness = one(*shards[0])
    for cut in shards[1:]:
        loudness = loudness * one(*cut)
    return loudness


def scatter_about(rng, shape, width, bound, split=(), held_as=jnp.bfloat16):
    result = width * jax.random.normal(rng, shape, jnp.float32)
    if split:
        result = result * levels(rng, shape, split, -0.22, 0.18)
    return jnp.clip(result, -bound, bound).astype(held_as)


def bell_draw_with(own_key, dims, deviation, limit, cuts, heavy, held_as=jnp.bfloat16):
    result = deviation * jax.random.normal(own_key, dims, jnp.float32)
    if cuts:
        result = result * levels(own_key, dims, cuts, -0.22, 0.18)
    return jnp.clip(with_spikes(result, jax.random.fold_in(own_key, 3), *heavy), -limit, limit).astype(held_as)


def setup_inputs(seed: int = 0) -> dict:
    key_list = jax.random.split(jax.random.key(seed), 9)
    return {
        "tokens": scatter_about(key_list[0], (TOKENS, D), 1.0, 6.0, ((0, 1024),)),
        "query_weight": scatter_about(key_list[1], (REPS, D, HD), D ** -0.5, 0.078125, ((0, 128), (1, 8))),
        "global_params": scatter_about(key_list[2], (D, C), 1.0, 6.0, ((0, 8),), jnp.float32),
        "local_params": bell_draw_with(key_list[3], (REPS, D, C), 1.0, 24.0, ((0, 128), (1, 8)), (0, 1, 128, 5.5)),
        "momentum": scatter_about(key_list[4], (FRAGS, D, C), 0.1, 0.6, ((1, 1024),), jnp.float32),
        "inner_steps": with_ends(jax.random.randint(key_list[5], (REPS,), 20, 101), jax.random.fold_in(key_list[5], 1), 20, 100).astype(jnp.int32),
        "replica_tokens": with_ends(jax.random.randint(key_list[6], (REPS,), 100000, 400001), jax.random.fold_in(key_list[6], 1), 100000, 400000).astype(jnp.int32),
        "plan": jax.random.randint(key_list[7], (1,), 0, FRAGS).astype(jnp.int32),
    }


decay_rate = 0.9
outer_rate = 0.7

def hadamard_table(order_n):
    row_ids = lax.broadcasted_iota(jnp.int32, (order_n, order_n), 0)
    col_ids = lax.broadcasted_iota(jnp.int32, (order_n, order_n), 1)
    common = jnp.bitwise_and(row_ids, col_ids)
    parity = jnp.zeros((order_n, order_n), jnp.int32)
    for bit_pos in range(order_n.bit_length() - 1):
        parity = parity + jnp.bitwise_and(jnp.right_shift(common, bit_pos), 1)
    signs = 1 - 2 * jnp.bitwise_and(parity, 1)
    return signs.astype(jnp.float32) / math.sqrt(order_n)

def transform(values, table):
    return jnp.einsum('rkb,bc->rkc', values, table, precision=lax.Precision.HIGHEST)

def reference(tokens, query_weight, global_params, local_params, momentum, inner_steps, replica_tokens, plan):
    grouped_tokens = tokens.reshape(REPS, TOKENS // REPS, D)

    def project(pair):
        return jnp.dot(pair[0], pair[1], preferred_element_type=jnp.float32)
    queries = lax.map(project, (grouped_tokens, query_weight))
    queries = queries.reshape(TOKENS, HD).astype(jnp.bfloat16)
    ratio = replica_tokens.astype(jnp.float32) / inner_steps.astype(jnp.float32)
    weights = ratio / jnp.sum(ratio)
    table = hadamard_table(BLOCK)

    def accumulate(total, item):
        local_one, weight_one = item
        delta = global_params - local_one.astype(jnp.float32)
        rotated = transform(delta.reshape(D, C // BLOCK, BLOCK), table)
        scale = lax.optimization_barrier(jnp.max(jnp.abs(rotated), axis=-1, keepdims=True)) + 1e-06
        code = lax.optimization_barrier((rotated / scale).astype(jnp.bfloat16))
        term = code.astype(jnp.float32) * scale * weight_one
        return (total + term, None)
    start_total = jnp.zeros((D, C // BLOCK, BLOCK), jnp.float32)
    total, _ = lax.scan(accumulate, start_total, (local_params, weights))
    average = transform(total, table).reshape(D, C)
    slot = lax.dynamic_index_in_dim(momentum, plan[0], 0, keepdims=False)
    new_momentum = decay_rate * slot + average
    new_params = global_params - outer_rate * (average + decay_rate * new_momentum)
    return (queries, new_params, new_momentum)
```

```python
import math

import jax
import jax.numpy as jnp
from jax import lax
from jax.experimental import pallas as pl
from jax.experimental.pallas import tpu as pltpu
from jax.sharding import PartitionSpec as P

BLOCK = 128
ROWS = 768
COLS = 256
GROUP = 48
OWN = 6
HALF = ROWS // 2
MESH = pl.DeviceIdType.MESH

decay_rate = 0.9
outer_rate = 0.7
keep = 1.0 - outer_rate * (1.0 + decay_rate)
root = 1.0 / math.sqrt(BLOCK)


def split3(values):
    high = values.astype(jnp.bfloat16)
    rest = values - high.astype(jnp.float32)
    middle = rest.astype(jnp.bfloat16)
    low = (rest - middle.astype(jnp.float32)).astype(jnp.bfloat16)
    return high, middle, low


def rotate(values, table):
    parts = [jnp.dot(part, table, preferred_element_type=jnp.float32) for part in split3(values)]
    return (parts[0] + parts[1] + parts[2]) * root


def kernel(
    tokens, query_weight, global_params, local_params, momentum, inner_steps, replica_tokens, plan,
    queries, residual, new_momentum,
    token_buf, weight_buf, global_buf, local_buf, momentum_buf, table_buf, term_buf,
    got1, send2, got2, slot_send, slot_got, moment_send, moment_got, send3, got3, gathered,
    load_sem, s1_send, s1_got, s2_send, s2_got, s3_send, s3_got, s4_send, s4_got, s5_send, s5_got,
    w_send, w_got, m_send, m_got,
):
    rep, shard = lax.axis_index("rep"), lax.axis_index("fsdp")
    core = lax.rem(rep, 2)
    z = lax.rem(rep // 2, 32)
    y = rep // 64
    ring = z // 4
    kind = lax.rem(rep, 8)
    group = 8 * y + kind
    twin = 64 * y + 8 * kind + ring
    paired = ring != kind
    x, y_hi = shard // 2, lax.rem(shard, 2)
    sign = 1 - 2 * lax.rem(z, 2)

    def at(dy, dz, dc):
        ny, nz, nc = lax.rem(y + dy, 2), lax.rem(z + dz + 32, 32), lax.rem(core + dc, 2)
        return 64 * ny + 2 * nz + nc, 8 * ny + 2 * lax.rem(nz, 4) + nc

    def around(step):
        return lax.rem(ring + step, 8)

    right, left = 2 * lax.rem(x + 1, 4) + y_hi, 2 * lax.rem(x + 3, 4) + y_hi
    across = 2 * x + 1 - y_hi

    loads = []
    for index, (source, target) in enumerate((
        (local_params.at[0], local_buf), (global_params, global_buf), (momentum, momentum_buf),
        (query_weight.at[0], weight_buf.at[shard]), (tokens, token_buf),
    )):
        loads.append(pltpu.make_async_copy(source, target, load_sem.at[index]))
        loads[-1].start()

    barrier = pltpu.get_barrier_semaphore()
    count = 0
    for dy in (0, 1):
        for dz in (0, 1, -1, 2, -2):
            for dc in (0, 1):
                if (dy, dz, dc) != (0, 0, 0):
                    pl.semaphore_signal(barrier, inc=1, device_id=(at(dy, dz, dc)[0], shard), device_id_type=MESH)
                    count += 1
    for step in range(1, 8):
        pl.semaphore_signal(
            barrier, inc=1, device_id=(64 * y + 8 * around(step) + kind, shard), device_id_type=MESH
        )
        count += 1
    for other in (right, left, across):
        pl.semaphore_signal(barrier, inc=1, device_id=(rep, other), device_id_type=MESH)
        count += 1

    @pl.when(paired)
    def _():
        pl.semaphore_signal(barrier, inc=1, device_id=(twin, shard), device_id_type=MESH)

    row = lax.broadcasted_iota(jnp.int32, (BLOCK, BLOCK), 0)
    col = lax.broadcasted_iota(jnp.int32, (BLOCK, BLOCK), 1)
    bits = row & col
    bits = bits ^ (bits >> 4)
    bits = bits ^ (bits >> 2)
    bits = bits ^ (bits >> 1)
    signs = (1 - 2 * (bits & 1)).astype(jnp.float32).astype(jnp.bfloat16)
    table_buf[...] = jnp.zeros_like(table_buf)
    table_buf[:BLOCK, :BLOCK] = signs
    table_buf[BLOCK:, BLOCK:] = signs

    ratio = replica_tokens[...].astype(jnp.float32) / inner_steps[...].astype(jnp.float32)
    lane = lax.broadcasted_iota(jnp.int32, (1, 128), 1)
    mine = jnp.sum(jnp.where(lane == rep, ratio, 0.0), axis=1, keepdims=True)
    share = mine / jnp.sum(ratio, axis=1, keepdims=True)

    loads[0].wait()
    loads[1].wait()

    def code_rows(step, carry):
        rows = pl.ds(pl.multiple_of(step * 192, 192), 192)
        delta = global_buf[rows, :] - local_buf[rows, :].astype(jnp.float32)
        rotated = rotate(delta, table_buf[...])
        for side in (0, 1):
            block = rotated[:, side * BLOCK:(side + 1) * BLOCK]
            scale = jnp.max(jnp.abs(block), axis=1, keepdims=True) + 1e-06
            code = (block / scale).astype(jnp.bfloat16)
            term = code.astype(jnp.float32) * scale * share
            term_buf[rows, side * BLOCK:(side + 1) * BLOCK] = term.astype(jnp.bfloat16)
        return carry

    lax.fori_loop(0, ROWS // 192, code_rows, 0)

    loads[2].wait()
    slot = momentum_buf[plan[0]]
    slot_send[...] = jnp.concatenate([slot[:, :BLOCK], slot[:, BLOCK:]], axis=0)

    pl.semaphore_wait(barrier, count + jnp.where(paired, 1, 0))

    def remote(source, target, sends, gots, index, device):
        return pltpu.make_async_remote_copy(
            src_ref=source, dst_ref=target, send_sem=sends.at[index], recv_sem=gots.at[index],
            device_id=device, device_id_type=MESH,
        )

    hops = (0, 1, -1, 2 * sign)
    window = [(dy, index, dc) for dy in (1, 0) for index in (3, 1, 2, 0) for dc in (1, 0)][:-1]
    first = []
    for dy, index, dc in window:
        device, rows = at(dy, hops[index], dc)
        place = 8 * dy + 2 * index + dc
        first.append(remote(
            term_buf.at[pl.ds(pl.multiple_of(rows * GROUP, GROUP), GROUP), :], got1.at[place],
            s1_send, s1_got, place, (device, shard),
        ))
        first[-1].start()

    own_weight = query_weight.at[0]
    ring1 = [
        remote(own_weight, weight_buf.at[shard], w_send, w_got, 0, (rep, right)),
        remote(own_weight, weight_buf.at[shard], w_send, w_got, 1, (rep, left)),
    ]
    for copy in ring1:
        copy.start()

    slot_copy = remote(slot_send, slot_got, m_send, m_got, 0, (twin, shard))

    @pl.when(paired)
    def _():
        slot_copy.start()

    @pl.when(jnp.logical_not(paired))
    def _():
        slot_got[...] = slot_send[...]

    loads[3].wait()
    loads[4].wait()

    def product(block):
        depth = pl.ds(pl.multiple_of(block * ROWS, ROWS), ROWS)
        return jnp.dot(token_buf[:, depth], weight_buf[block], preferred_element_type=jnp.float32)

    total = product(shard)

    own_rows = global_buf[pl.ds(pl.multiple_of(group * GROUP, GROUP), GROUP), :]
    own_global = jnp.zeros((OWN, COLS), jnp.float32)
    for index in range(8):
        own_global = own_global + jnp.where(ring == index, own_rows[OWN * index:OWN * (index + 1), :], 0.0)
    own_global = jnp.concatenate([own_global[:, :BLOCK], own_global[:, BLOCK:]], axis=0)

    summed = term_buf[pl.ds(pl.multiple_of(group * GROUP, GROUP), GROUP), :].astype(jnp.float32)
    for (dy, index, dc), copy in reversed(list(zip(window, first))):
        copy.wait_recv()
        summed = summed + got1[8 * dy + 2 * index + dc].astype(jnp.float32)
    for index in range(8):
        send2[index, :OWN, :] = summed[OWN * index:OWN * (index + 1), :BLOCK]
        send2[index, OWN:, :] = summed[OWN * index:OWN * (index + 1), BLOCK:]

    order = (4, 3, 5, 2, 6, 1, 7)
    second = []
    for step in order:
        other = around(step)
        second.append(remote(
            send2.at[other], got2.at[step], s2_send, s2_got, step, (64 * y + 8 * other + kind, shard),
        ))
        second[-1].start()

    across_copy = remote(own_weight, weight_buf.at[shard], w_send, w_got, 4, (rep, across))
    across_copy.start()

    block_left, block_right = left, right

    def forward(block_from_left, block_from_right, base):
        top, bottom = pl.ds(0, HALF), pl.ds(HALF, HALF)
        return [
            remote(weight_buf.at[block_from_left, top, :], weight_buf.at[block_from_left, top, :],
                   w_send, w_got, base, (rep, right)),
            remote(weight_buf.at[block_from_right, bottom, :], weight_buf.at[block_from_right, bottom, :],
                   w_send, w_got, base + 1, (rep, left)),
        ]

    for copy in ring1:
        copy.wait_recv()
    ring2 = forward(block_left, block_right, 2)
    for copy in ring2:
        copy.start()
    total = total + product(left) + product(right)

    @pl.when(paired)
    def _():
        slot_copy.wait_recv()

    owned = send2[ring]
    for step, copy in reversed(list(zip(order, second))):
        copy.wait_recv()
        owned = owned + got2[step]
    average = rotate(owned, table_buf[:BLOCK, :BLOCK])
    moment = decay_rate * slot_got[...] + average
    moment_send[...] = moment
    rest = (1.0 - keep) * own_global - outer_rate * (average + decay_rate * moment)
    send3[:2 * OWN, :] = rest
    send3[2 * OWN:, :] = jnp.zeros((4, BLOCK), jnp.float32)
    got3[ring] = send3[...].astype(jnp.bfloat16)

    third = []
    for step in order:
        other = around(step)
        third.append(remote(
            got3.at[ring], got3.at[ring], s3_send, s3_got, step, (64 * y + 8 * other + kind, shard),
        ))
        third[-1].start()
    moment_copy = remote(moment_send, moment_got, m_send, m_got, 1, (twin, shard))

    @pl.when(paired)
    def _():
        moment_copy.start()

    @pl.when(jnp.logical_not(paired))
    def _():
        moment_got[...] = moment_send[...]

    across_copy.wait_recv()
    ring3 = [
        remote(weight_buf.at[across], weight_buf.at[across], w_send, w_got, 5, (rep, right)),
        remote(weight_buf.at[across], weight_buf.at[across], w_send, w_got, 6, (rep, left)),
    ]
    for copy in ring3:
        copy.start()
    far = 2 * lax.rem(x + 2, 4) + y_hi
    for copy in ring2:
        copy.wait_recv()
    total = total + product(across) + product(far)

    for copy in reversed(third):
        copy.wait_recv()
    pieces = got3[...].astype(jnp.float32)
    whole = jnp.concatenate([
        jnp.concatenate([pieces[index, :OWN, :] for index in range(8)], axis=0),
        jnp.concatenate([pieces[index, OWN:2 * OWN, :] for index in range(8)], axis=0),
    ], axis=1)
    gathered[pl.ds(pl.multiple_of(group * GROUP, GROUP), GROUP), :] = whole.astype(jnp.bfloat16)

    def rows_of(number):
        return gathered.at[pl.ds(pl.multiple_of(number * GROUP, GROUP), GROUP), :]

    near = [(dy, index) for dy in (1, 0) for index in (3, 1, 2, 0)][:-1]
    fourth = []
    for dy, index in near:
        fourth.append(remote(
            rows_of(group), rows_of(group), s4_send, s4_got, 4 * dy + index,
            (at(dy, -hops[index], 0)[0], shard),
        ))
        fourth[-1].start()
    sibling = at(0, 0, 1)[0]
    fifth = [remote(rows_of(group), rows_of(group), s5_send, s5_got, 0, (sibling, shard))]
    fifth[0].start()

    for copy in ring3:
        copy.wait_recv()
    across_left, across_right = 2 * lax.rem(x + 3, 4) + 1 - y_hi, 2 * lax.rem(x + 1, 4) + 1 - y_hi
    ring4 = forward(across_left, across_right, 7)
    for copy in ring4:
        copy.start()
    total = total + product(across_left) + product(across_right)

    @pl.when(paired)
    def _():
        moment_copy.wait_recv()

    new_momentum[...] = jnp.concatenate([moment_got[:OWN, :], moment_got[OWN:, :]], axis=1)

    for (dy, index), copy in reversed(list(zip(near, fourth))):
        copy.wait_recv()
        number = at(dy, hops[index], 0)[1]
        fifth.append(remote(
            rows_of(number), rows_of(number), s5_send, s5_got, 4 * dy + index, (sibling, shard),
        ))
        fifth[-1].start()
    for copy in ring4:
        copy.wait_recv()
    total = total + product(2 * lax.rem(x + 2, 4) + 1 - y_hi)
    queries[...] = total.astype(jnp.bfloat16)
    for copy in fifth:
        copy.wait_recv()
    residual[...] = gathered[...]

    for copy in first + ring1 + second + [across_copy] + ring2 + third + ring3 + fourth + ring4 + fifth:
        copy.wait_send()

    @pl.when(paired)
    def _():
        slot_copy.wait_send()
        moment_copy.wait_send()


def local(
    tokens, query_weight, global_params, local_params, momentum, inner_steps, replica_tokens, plan
):
    anywhere = pl.BlockSpec(memory_space=pl.ANY)
    vmem = pl.BlockSpec(memory_space=pltpu.VMEM)
    smem = pl.BlockSpec(memory_space=pltpu.SMEM)
    dma = pltpu.SemaphoreType.DMA
    f32, bf16 = jnp.float32, jnp.bfloat16
    queries, residual, new_momentum = pl.pallas_call(
        kernel,
        out_shape=(
            jax.ShapeDtypeStruct((224, 128), bf16),
            jax.ShapeDtypeStruct((ROWS, COLS), bf16),
            jax.ShapeDtypeStruct((OWN, COLS), f32),
        ),
        in_specs=[anywhere] * 5 + [vmem, vmem, smem],
        out_specs=(vmem, vmem, vmem),
        scratch_shapes=[
            pltpu.VMEM((224, 6144), bf16),
            pltpu.VMEM((8, ROWS, 128), bf16),
            pltpu.VMEM((ROWS, COLS), f32),
            pltpu.VMEM((ROWS, COLS), bf16),
            pltpu.VMEM((8, OWN, COLS), f32),
            pltpu.VMEM((COLS, COLS), bf16),
            pltpu.VMEM((ROWS, COLS), bf16),
            pltpu.VMEM((16, GROUP, COLS), bf16),
            pltpu.VMEM((8, 2 * OWN, BLOCK), f32),
            pltpu.VMEM((8, 2 * OWN, BLOCK), f32),
            pltpu.VMEM((2 * OWN, BLOCK), f32),
            pltpu.VMEM((2 * OWN, BLOCK), f32),
            pltpu.VMEM((2 * OWN, BLOCK), f32),
            pltpu.VMEM((2 * OWN, BLOCK), f32),
            pltpu.VMEM((16, BLOCK), f32),
            pltpu.VMEM((8, 16, BLOCK), bf16),
            pltpu.VMEM((ROWS, COLS), bf16),
            dma((5,)),
            dma((16,)), dma((16,)),
            dma((8,)), dma((8,)),
            dma((8,)), dma((8,)),
            dma((8,)), dma((8,)),
            dma((8,)), dma((8,)),
            dma((9,)), dma((9,)),
            dma((2,)), dma((2,)),
        ],
        compiler_params=pltpu.CompilerParams(
            collective_id=0, has_side_effects=True, vmem_limit_bytes=32 * 1024 * 1024
        ),
        name="outer_step",
    )(
        tokens, query_weight, global_params, local_params, momentum,
        inner_steps.reshape(1, 128), replica_tokens.reshape(1, 128), plan,
    )
    new_params = keep * global_params + residual.astype(f32)
    return queries, new_params, new_momentum


def solution(mesh):
    return jax.shard_map(
        local,
        mesh=mesh,
        in_specs=(
            P(("rep", "fsdp"), None),
            P("rep", "fsdp", None),
            P("fsdp", None),
            P("rep", "fsdp", None),
            P(None, ("fsdp", "rep"), None),
            P(),
            P(),
            P(),
        ),
        out_specs=(P(("rep", "fsdp"), None), P("fsdp", None), P(("fsdp", "rep"), None)),
        check_vma=False,
    )
```

```python
import math

import jax
import jax.numpy as jnp
from jax import lax
from jax.experimental import pallas as pl
from jax.experimental.pallas import tpu as pltpu
from jax.sharding import PartitionSpec as P

BLOCK = 128
ROWS = 768
COLS = 256
GROUP = 48
OWN = 6
HALF = ROWS // 2
MESH = pl.DeviceIdType.MESH

decay_rate = 0.9
outer_rate = 0.7
keep = 1.0 - outer_rate * (1.0 + decay_rate)
slot_share = decay_rate * decay_rate / (1.0 + decay_rate)
root = 1.0 / math.sqrt(BLOCK)


def split3(values):
    high = values.astype(jnp.bfloat16)
    rest = values - high.astype(jnp.float32)
    middle = rest.astype(jnp.bfloat16)
    low = (rest - middle.astype(jnp.float32)).astype(jnp.bfloat16)
    return high, middle, low


def rotate(values, table):
    parts = [jnp.dot(part, table, preferred_element_type=jnp.float32) for part in split3(values)]
    return (parts[0] + parts[1] + parts[2]) * root


def kernel(
    tokens, query_weight, global_params, local_params, momentum, inner_steps, replica_tokens, plan,
    queries, residual, new_momentum,
    token_buf, weight_buf, global_buf, local_buf, momentum_buf, table_buf, term_buf,
    got1, send2, got2, moment_send, moment_got, send3, got3, gathered,
    load_sem, s1_send, s1_got, s2_send, s2_got, s3_send, s3_got, s4_send, s4_got, s5_send, s5_got,
    w_send, w_got, m_send, m_got, far_sem,
):
    rep, shard = lax.axis_index("rep"), lax.axis_index("fsdp")
    core = lax.rem(rep, 2)
    z = lax.rem(rep // 2, 32)
    y = rep // 64
    ring = z // 4
    kind = lax.rem(rep, 8)
    group = 8 * y + kind
    twin = 64 * y + 8 * kind + ring
    paired = ring != kind
    chunk = 8 * y + ring
    x, y_hi = shard // 2, lax.rem(shard, 2)
    sign = 1 - 2 * lax.rem(z, 2)

    def at(dy, dz, dc):
        ny, nz, nc = lax.rem(y + dy, 2), lax.rem(z + dz + 32, 32), lax.rem(core + dc, 2)
        return 64 * ny + 2 * nz + nc, 8 * ny + 2 * lax.rem(nz, 4) + nc

    def around(step):
        return lax.rem(ring + step, 8)

    right, left = 2 * lax.rem(x + 1, 4) + y_hi, 2 * lax.rem(x + 3, 4) + y_hi
    across = 2 * x + 1 - y_hi

    loads = []
    for index, (source, target) in enumerate((
        (local_params.at[0], local_buf), (global_params, global_buf), (momentum, momentum_buf),
        (query_weight.at[0], weight_buf.at[shard]), (tokens, token_buf),
    )):
        loads.append(pltpu.make_async_copy(source, target, load_sem.at[index]))
        loads[-1].start()

    barrier = pltpu.get_barrier_semaphore()
    count = 0
    for dy in (0, 1):
        for dz in (0, 1, -1, 2, -2):
            for dc in (0, 1):
                if (dy, dz, dc) != (0, 0, 0):
                    pl.semaphore_signal(barrier, inc=1, device_id=(at(dy, dz, dc)[0], shard), device_id_type=MESH)
                    count += 1
    for dz in (4, -4, 8, -8):
        pl.semaphore_signal(barrier, inc=1, device_id=(at(0, dz, 0)[0], shard), device_id_type=MESH)
        count += 1
    for other in (right, left, across):
        pl.semaphore_signal(barrier, inc=1, device_id=(rep, other), device_id_type=MESH)
        count += 1

    row = lax.broadcasted_iota(jnp.int32, (BLOCK, BLOCK), 0)
    col = lax.broadcasted_iota(jnp.int32, (BLOCK, BLOCK), 1)
    bits = row & col
    bits = bits ^ (bits >> 4)
    bits = bits ^ (bits >> 2)
    bits = bits ^ (bits >> 1)
    signs = (1 - 2 * (bits & 1)).astype(jnp.float32).astype(jnp.bfloat16)
    table_buf[...] = jnp.zeros_like(table_buf)
    table_buf[:BLOCK, :BLOCK] = signs
    table_buf[BLOCK:, BLOCK:] = signs

    ratio = replica_tokens[...].astype(jnp.float32) / inner_steps[...].astype(jnp.float32)
    lane = lax.broadcasted_iota(jnp.int32, (1, 128), 1)
    mine = jnp.sum(jnp.where(lane == rep, ratio, 0.0), axis=1, keepdims=True)
    share = mine / jnp.sum(ratio, axis=1, keepdims=True)

    loads[0].wait()
    loads[1].wait()

    def code_rows(step, carry):
        rows = pl.ds(pl.multiple_of(step * 192, 192), 192)
        delta = global_buf[rows, :] - local_buf[rows, :].astype(jnp.float32)
        rotated = rotate(delta, table_buf[...])
        for side in (0, 1):
            block = rotated[:, side * BLOCK:(side + 1) * BLOCK]
            scale = jnp.max(jnp.abs(block), axis=1, keepdims=True) + 1e-06
            code = (block / scale).astype(jnp.bfloat16)
            term = code.astype(jnp.float32) * scale * share
            term_buf[rows, side * BLOCK:(side + 1) * BLOCK] = term.astype(jnp.bfloat16)
        return carry

    lax.fori_loop(0, ROWS // 192, code_rows, 0)

    loads[2].wait()
    fragment = lax.broadcasted_iota(jnp.int32, momentum_buf.shape, 1)
    slot = jnp.sum(jnp.where(fragment == plan[0], momentum_buf[...], 0.0), axis=1)
    spread = jnp.concatenate([jnp.where(kind == index, slot, 0.0) for index in range(8)], axis=0)
    chunk_rows = pl.ds(pl.multiple_of(chunk * GROUP, GROUP), GROUP)
    shifted = term_buf[chunk_rows, :].astype(jnp.float32) + slot_share * rotate(spread, table_buf[...])
    term_buf[chunk_rows, :] = shifted.astype(jnp.bfloat16)

    pl.semaphore_wait(barrier, count)
    for dz in (8, -8):
        pl.semaphore_signal(far_sem, inc=1, device_id=(at(0, dz, 0)[0], shard), device_id_type=MESH)

    def remote(source, target, sends, gots, index, device):
        return pltpu.make_async_remote_copy(
            src_ref=source, dst_ref=target, send_sem=sends.at[index], recv_sem=gots.at[index],
            device_id=device, device_id_type=MESH,
        )

    hops = (0, 1, -1, 2 * sign)
    window = [(dy, index, dc) for dy in (1, 0) for index in (3, 1, 2, 0) for dc in (1, 0)][:-1]
    first = []
    for dy, index, dc in window:
        device, rows = at(dy, hops[index], dc)
        place = 8 * dy + 2 * index + dc
        first.append(remote(
            term_buf.at[pl.ds(pl.multiple_of(rows * GROUP, GROUP), GROUP), :], got1.at[place],
            s1_send, s1_got, place, (device, shard),
        ))
        first[-1].start()

    own_weight = query_weight.at[0]
    ring1 = [
        remote(own_weight, weight_buf.at[shard], w_send, w_got, 0, (rep, right)),
        remote(own_weight, weight_buf.at[shard], w_send, w_got, 1, (rep, left)),
    ]
    for copy in ring1:
        copy.start()

    loads[3].wait()
    loads[4].wait()

    def product(block):
        depth = pl.ds(pl.multiple_of(block * ROWS, ROWS), ROWS)
        return jnp.dot(token_buf[:, depth], weight_buf[block], preferred_element_type=jnp.float32)

    total = product(shard)

    own_rows = global_buf[pl.ds(pl.multiple_of(group * GROUP, GROUP), GROUP), :]
    own_global = jnp.zeros((OWN, COLS), jnp.float32)
    for index in range(8):
        own_global = own_global + jnp.where(ring == index, own_rows[OWN * index:OWN * (index + 1), :], 0.0)
    own_global = jnp.concatenate([own_global[:, :BLOCK], own_global[:, BLOCK:]], axis=0)

    summed = term_buf[pl.ds(pl.multiple_of(group * GROUP, GROUP), GROUP), :].astype(jnp.float32)
    for (dy, index, dc), copy in reversed(list(zip(window, first))):
        copy.wait_recv()
        summed = summed + got1[8 * dy + 2 * index + dc].astype(jnp.float32)
    for index in range(8):
        send2[index, :OWN, :] = summed[OWN * index:OWN * (index + 1), :BLOCK]
        send2[index, OWN:, :] = summed[OWN * index:OWN * (index + 1), BLOCK:]

    order = (4, 3, 5, 2, 6, 1, 7)
    pl.semaphore_wait(far_sem, 2)
    second = []
    for step in order:
        other = around(step)
        second.append(remote(
            send2.at[other], got2.at[step], s2_send, s2_got, step, (64 * y + 8 * other + kind, shard),
        ))
        second[-1].start()

    across_copy = remote(own_weight, weight_buf.at[shard], w_send, w_got, 4, (rep, across))
    across_copy.start()

    block_left, block_right = left, right

    def forward(block_from_left, block_from_right, base):
        top, bottom = pl.ds(0, HALF), pl.ds(HALF, HALF)
        return [
            remote(weight_buf.at[block_from_left, top, :], weight_buf.at[block_from_left, top, :],
                   w_send, w_got, base, (rep, right)),
            remote(weight_buf.at[block_from_right, bottom, :], weight_buf.at[block_from_right, bottom, :],
                   w_send, w_got, base + 1, (rep, left)),
        ]

    for copy in ring1:
        copy.wait_recv()
    ring2 = forward(block_left, block_right, 2)
    for copy in ring2:
        copy.start()
    total = total + product(left) + product(right)

    owned = send2[ring]
    for step, copy in reversed(list(zip(order, second))):
        copy.wait_recv()
        owned = owned + got2[step]
    average = rotate(owned, table_buf[:BLOCK, :BLOCK])
    moment_send[...] = average
    rest = (1.0 - keep) * (own_global - average)
    send3[:2 * OWN, :] = rest
    send3[2 * OWN:, :] = jnp.zeros((4, BLOCK), jnp.float32)
    got3[ring] = send3[...].astype(jnp.bfloat16)

    third = []
    for step in order:
        other = around(step)
        third.append(remote(
            got3.at[ring], got3.at[ring], s3_send, s3_got, step, (64 * y + 8 * other + kind, shard),
        ))
        third[-1].start()
    moment_copy = remote(moment_send, moment_got, m_send, m_got, 0, (twin, shard))

    @pl.when(paired)
    def _():
        moment_copy.start()

    @pl.when(jnp.logical_not(paired))
    def _():
        moment_got[...] = moment_send[...]

    across_copy.wait_recv()
    ring3 = [
        remote(weight_buf.at[across], weight_buf.at[across], w_send, w_got, 5, (rep, right)),
        remote(weight_buf.at[across], weight_buf.at[across], w_send, w_got, 6, (rep, left)),
    ]
    for copy in ring3:
        copy.start()
    far = 2 * lax.rem(x + 2, 4) + y_hi
    for copy in ring2:
        copy.wait_recv()
    total = total + product(across) + product(far)

    for copy in reversed(third):
        copy.wait_recv()
    pieces = got3[...].astype(jnp.float32)
    whole = jnp.concatenate([
        jnp.concatenate([pieces[index, :OWN, :] for index in range(8)], axis=0),
        jnp.concatenate([pieces[index, OWN:2 * OWN, :] for index in range(8)], axis=0),
    ], axis=1)
    gathered[pl.ds(pl.multiple_of(group * GROUP, GROUP), GROUP), :] = whole.astype(jnp.bfloat16)

    def rows_of(number):
        return gathered.at[pl.ds(pl.multiple_of(number * GROUP, GROUP), GROUP), :]

    near = [(dy, index) for dy in (1, 0) for index in (3, 1, 2, 0)][:-1]
    fourth = []
    for dy, index in near:
        fourth.append(remote(
            rows_of(group), rows_of(group), s4_send, s4_got, 4 * dy + index,
            (at(dy, -hops[index], 0)[0], shard),
        ))
        fourth[-1].start()
    sibling = at(0, 0, 1)[0]
    fifth = [remote(rows_of(group), rows_of(group), s5_send, s5_got, 0, (sibling, shard))]
    fifth[0].start()

    for copy in ring3:
        copy.wait_recv()
    across_left, across_right = 2 * lax.rem(x + 3, 4) + 1 - y_hi, 2 * lax.rem(x + 1, 4) + 1 - y_hi
    ring4 = forward(across_left, across_right, 7)
    for copy in ring4:
        copy.start()
    total = total + product(across_left) + product(across_right)

    @pl.when(paired)
    def _():
        moment_copy.wait_recv()

    shifted_rows = jnp.concatenate([moment_got[:OWN, :], moment_got[OWN:, :]], axis=1)
    new_momentum[...] = shifted_rows + (decay_rate - slot_share) * slot

    for (dy, index), copy in reversed(list(zip(near, fourth))):
        copy.wait_recv()
        number = at(dy, hops[index], 0)[1]
        fifth.append(remote(
            rows_of(number), rows_of(number), s5_send, s5_got, 4 * dy + index, (sibling, shard),
        ))
        fifth[-1].start()
    for copy in ring4:
        copy.wait_recv()
    total = total + product(2 * lax.rem(x + 2, 4) + 1 - y_hi)
    queries[...] = total.astype(jnp.bfloat16)
    for copy in fifth:
        copy.wait_recv()
    residual[...] = gathered[...]

    for copy in first + ring1 + second + [across_copy] + ring2 + third + ring3 + fourth + ring4 + fifth:
        copy.wait_send()

    @pl.when(paired)
    def _():
        moment_copy.wait_send()


def local(
    tokens, query_weight, global_params, local_params, momentum, inner_steps, replica_tokens, plan
):
    anywhere = pl.BlockSpec(memory_space=pl.ANY)
    vmem = pl.BlockSpec(memory_space=pltpu.VMEM)
    smem = pl.BlockSpec(memory_space=pltpu.SMEM)
    dma = pltpu.SemaphoreType.DMA
    f32, bf16 = jnp.float32, jnp.bfloat16
    queries, residual, new_momentum = pl.pallas_call(
        kernel,
        out_shape=(
            jax.ShapeDtypeStruct((224, 128), bf16),
            jax.ShapeDtypeStruct((ROWS, COLS), bf16),
            jax.ShapeDtypeStruct((OWN, COLS), f32),
        ),
        in_specs=[anywhere] * 5 + [vmem, vmem, smem],
        out_specs=(vmem, vmem, vmem),
        scratch_shapes=[
            pltpu.VMEM((224, 6144), bf16),
            pltpu.VMEM((8, ROWS, 128), bf16),
            pltpu.VMEM((ROWS, COLS), f32),
            pltpu.VMEM((ROWS, COLS), bf16),
            pltpu.VMEM((OWN, 8, COLS), f32),
            pltpu.VMEM((COLS, COLS), bf16),
            pltpu.VMEM((ROWS, COLS), bf16),
            pltpu.VMEM((16, GROUP, COLS), bf16),
            pltpu.VMEM((8, 2 * OWN, BLOCK), f32),
            pltpu.VMEM((8, 2 * OWN, BLOCK), f32),
            pltpu.VMEM((2 * OWN, BLOCK), f32),
            pltpu.VMEM((2 * OWN, BLOCK), f32),
            pltpu.VMEM((16, BLOCK), f32),
            pltpu.VMEM((8, 16, BLOCK), bf16),
            pltpu.VMEM((ROWS, COLS), bf16),
            dma((5,)),
            dma((16,)), dma((16,)),
            dma((8,)), dma((8,)),
            dma((8,)), dma((8,)),
            dma((8,)), dma((8,)),
            dma((8,)), dma((8,)),
            dma((9,)), dma((9,)),
            dma((1,)), dma((1,)),
            pltpu.SemaphoreType.REGULAR,
        ],
        compiler_params=pltpu.CompilerParams(
            collective_id=0, has_side_effects=True, vmem_limit_bytes=60 * 1024 * 1024
        ),
        name="outer_step",
    )(
        tokens, query_weight, global_params, local_params, momentum.transpose(1, 0, 2),
        inner_steps.reshape(1, 128), replica_tokens.reshape(1, 128), plan,
    )
    new_params = keep * global_params + residual.astype(f32)
    return queries, new_params, new_momentum


def solution(mesh):
    return jax.shard_map(
        local,
        mesh=mesh,
        in_specs=(
            P(("rep", "fsdp"), None),
            P("rep", "fsdp", None),
            P("fsdp", None),
            P("rep", "fsdp", None),
            P(None, ("fsdp", "rep"), None),
            P(),
            P(),
            P(),
        ),
        out_specs=(P(("rep", "fsdp"), None), P("fsdp", None), P(("fsdp", "rep"), None)),
        check_vma=False,
    )
```

```python
import math

import jax
import jax.numpy as jnp
from jax import lax
from jax.experimental import pallas as pl
from jax.experimental.pallas import tpu as pltpu
from jax.sharding import PartitionSpec as P

BLOCK = 128
ROWS = 768
COLS = 256
GROUP = 48
OWN = 6
HALF = ROWS // 2
MESH = pl.DeviceIdType.MESH

decay_rate = 0.9
outer_rate = 0.7
keep = 1.0 - outer_rate * (1.0 + decay_rate)
slot_share = decay_rate * decay_rate / (1.0 + decay_rate)
root = 1.0 / math.sqrt(BLOCK)


def split3(values):
    high = values.astype(jnp.bfloat16)
    rest = values - high.astype(jnp.float32)
    middle = rest.astype(jnp.bfloat16)
    low = (rest - middle.astype(jnp.float32)).astype(jnp.bfloat16)
    return high, middle, low


def rotate(values, table):
    parts = [jnp.dot(part, table, preferred_element_type=jnp.float32) for part in split3(values)]
    return (parts[0] + parts[1] + parts[2]) * root


def kernel(
    tokens, query_weight, global_params, local_params, momentum, inner_steps, replica_tokens, plan,
    queries, residual, new_momentum,
    token_buf, weight_buf, global_buf, local_buf, momentum_buf, table_buf, term_buf, steps_buf, trained_buf,
    got1, far_send, far_got, moment_send, moment_got, gathered,
    load_sem, s1_send, s1_got, s2_send, s2_got, s3_send, s3_got, s4_send, s4_got, s5_send, s5_got,
    w_send, w_got, m_send, m_got,
):
    rep, shard = lax.axis_index("rep"), lax.axis_index("fsdp")
    core = lax.rem(rep, 2)
    z = lax.rem(rep // 2, 32)
    y = rep // 64
    ring = z // 4
    kind = lax.rem(rep, 8)
    group = 8 * y + kind
    hub = ring == 0
    chunk = 8 * y + ring
    x, y_hi = shard // 2, lax.rem(shard, 2)
    sign = 1 - 2 * lax.rem(z, 2)

    def at(dy, dz, dc):
        ny, nz, nc = lax.rem(y + dy, 2), lax.rem(z + dz + 32, 32), lax.rem(core + dc, 2)
        return 64 * ny + 2 * nz + nc, 8 * ny + 2 * lax.rem(nz, 4) + nc

    right, left = 2 * lax.rem(x + 1, 4) + y_hi, 2 * lax.rem(x + 3, 4) + y_hi
    across = 2 * x + 1 - y_hi

    loads = []
    for index, (source, target) in enumerate((
        (local_params.at[0], local_buf), (global_params, global_buf), (momentum, momentum_buf),
        (query_weight.at[0], weight_buf.at[shard]), (tokens, token_buf),
        (inner_steps, steps_buf), (replica_tokens, trained_buf),
    )):
        loads.append(pltpu.make_async_copy(source, target, load_sem.at[index]))
        loads[-1].start()

    barrier = pltpu.get_barrier_semaphore()
    count = 0
    for dy in (0, 1):
        for dz in (0, 1, -1, 2, -2):
            for dc in (0, 1):
                if (dy, dz, dc) != (0, 0, 0):
                    pl.semaphore_signal(barrier, inc=1, device_id=(at(dy, dz, dc)[0], shard), device_id_type=MESH)
                    count += 1
    for other in (right, left, across):
        pl.semaphore_signal(barrier, inc=1, device_id=(rep, other), device_id_type=MESH)
        count += 1

    @pl.when(hub)
    def _():
        for step in range(1, 8):
            pl.semaphore_signal(barrier, inc=1, device_id=(64 * y + 8 * step + kind, shard), device_id_type=MESH)

    row = lax.broadcasted_iota(jnp.int32, (BLOCK, BLOCK), 0)
    col = lax.broadcasted_iota(jnp.int32, (BLOCK, BLOCK), 1)
    bits = row & col
    bits = bits ^ (bits >> 4)
    bits = bits ^ (bits >> 2)
    bits = bits ^ (bits >> 1)
    signs = (1 - 2 * (bits & 1)).astype(jnp.float32).astype(jnp.bfloat16)
    table_buf[...] = jnp.zeros_like(table_buf)
    table_buf[:BLOCK, :BLOCK] = signs
    table_buf[BLOCK:, BLOCK:] = signs

    loads[5].wait()
    loads[6].wait()
    ratio = trained_buf[...].astype(jnp.float32) / steps_buf[...].astype(jnp.float32)
    lane = lax.broadcasted_iota(jnp.int32, (1, 128), 1)
    mine = jnp.sum(jnp.where(lane == rep, ratio, 0.0), axis=1, keepdims=True)
    share = mine / jnp.sum(ratio, axis=1, keepdims=True)

    loads[0].wait()
    loads[1].wait()

    def code_rows(step, carry):
        rows = pl.ds(pl.multiple_of(step * 192, 192), 192)
        delta = global_buf[rows, :] - local_buf[rows, :].astype(jnp.float32)
        rotated = rotate(delta, table_buf[...])
        for side in (0, 1):
            block = rotated[:, side * BLOCK:(side + 1) * BLOCK]
            scale = jnp.max(jnp.abs(block), axis=1, keepdims=True) + 1e-06
            code = (block / scale).astype(jnp.bfloat16)
            term = code.astype(jnp.float32) * scale * share
            term_buf[rows, side * BLOCK:(side + 1) * BLOCK] = term.astype(jnp.bfloat16)
        return carry

    lax.fori_loop(0, ROWS // 192, code_rows, 0)

    loads[2].wait()
    fragment = lax.broadcasted_iota(jnp.int32, momentum_buf.shape, 1)
    slot = jnp.sum(jnp.where(fragment == plan[0], momentum_buf[...], 0.0), axis=1)
    spread = jnp.concatenate([jnp.where(kind == index, slot, 0.0) for index in range(8)], axis=0)
    chunk_rows = pl.ds(pl.multiple_of(chunk * GROUP, GROUP), GROUP)
    shifted = term_buf[chunk_rows, :].astype(jnp.float32) + slot_share * rotate(spread, table_buf[...])
    term_buf[chunk_rows, :] = shifted.astype(jnp.bfloat16)

    pl.semaphore_wait(barrier, count + jnp.where(hub, 0, 1))

    def remote(source, target, sends, gots, index, device):
        return pltpu.make_async_remote_copy(
            src_ref=source, dst_ref=target, send_sem=sends.at[index], recv_sem=gots.at[index],
            device_id=device, device_id_type=MESH,
        )

    hops = (0, 1, -1, 2 * sign)
    window = [(dy, index, dc) for dy in (1, 0) for index in (3, 1, 2, 0) for dc in (1, 0)][:-1]
    first = []
    for dy, index, dc in window:
        device, rows = at(dy, hops[index], dc)
        place = 8 * dy + 2 * index + dc
        first.append(remote(
            term_buf.at[pl.ds(pl.multiple_of(rows * GROUP, GROUP), GROUP), :], got1.at[place],
            s1_send, s1_got, place, (device, shard),
        ))
        first[-1].start()

    own_weight = query_weight.at[0]
    ring1 = [
        remote(own_weight, weight_buf.at[shard], w_send, w_got, 0, (rep, right)),
        remote(own_weight, weight_buf.at[shard], w_send, w_got, 1, (rep, left)),
    ]
    for copy in ring1:
        copy.start()

    loads[3].wait()
    loads[4].wait()

    def product(block):
        depth = pl.ds(pl.multiple_of(block * ROWS, ROWS), ROWS)
        return jnp.dot(token_buf[:, depth], weight_buf[block], preferred_element_type=jnp.float32)

    total = product(shard)

    summed = term_buf[pl.ds(pl.multiple_of(group * GROUP, GROUP), GROUP), :].astype(jnp.float32)
    for (dy, index, dc), copy in reversed(list(zip(window, first))):
        copy.wait_recv()
        summed = summed + got1[8 * dy + 2 * index + dc].astype(jnp.float32)
    far_send[...] = summed

    def to_hub(index):
        return remote(far_send, far_got.at[index], s2_send, s2_got, index, (64 * y + kind, shard))

    @pl.when(jnp.logical_not(hub))
    def _():
        to_hub(ring).start()

    across_copy = remote(own_weight, weight_buf.at[shard], w_send, w_got, 4, (rep, across))
    across_copy.start()

    block_left, block_right = left, right

    def forward(block_from_left, block_from_right, base):
        top, bottom = pl.ds(0, HALF), pl.ds(HALF, HALF)
        return [
            remote(weight_buf.at[block_from_left, top, :], weight_buf.at[block_from_left, top, :],
                   w_send, w_got, base, (rep, right)),
            remote(weight_buf.at[block_from_right, bottom, :], weight_buf.at[block_from_right, bottom, :],
                   w_send, w_got, base + 1, (rep, left)),
        ]

    for copy in ring1:
        copy.wait_recv()
    ring2 = forward(block_left, block_right, 2)
    for copy in ring2:
        copy.start()
    total = total + product(left) + product(right)

    across_copy.wait_recv()
    ring3 = [
        remote(weight_buf.at[across], weight_buf.at[across], w_send, w_got, 5, (rep, right)),
        remote(weight_buf.at[across], weight_buf.at[across], w_send, w_got, 6, (rep, left)),
    ]
    for copy in ring3:
        copy.start()
    far = 2 * lax.rem(x + 2, 4) + y_hi
    for copy in ring2:
        copy.wait_recv()
    total = total + product(across) + product(far)

    def rows_of(number):
        return gathered.at[pl.ds(pl.multiple_of(number * GROUP, GROUP), GROUP), :]

    def to_ring(index):
        return remote(rows_of(group), rows_of(group), s3_send, s3_got, index, (64 * y + 8 * index + kind, shard))

    @pl.when(hub)
    def _():
        summed = far_send[...]
        for index in (1, 2, 3, 7, 6, 5, 4):
            to_hub(index).wait_recv()
            summed = summed + far_got[index]
        average = rotate(summed, table_buf[...])
        for index in range(8):
            moment_send[index] = average[OWN * index:OWN * (index + 1), :]
        own_global = global_buf[pl.ds(pl.multiple_of(group * GROUP, GROUP), GROUP), :]
        rest = (1.0 - keep) * (own_global - average)
        gathered[pl.ds(pl.multiple_of(group * GROUP, GROUP), GROUP), :] = rest.astype(jnp.bfloat16)
        to_ring(1).start()

    @pl.when(jnp.logical_not(hub))
    def _():
        to_ring(ring).wait_recv()

    spot = lax.rem(z, 4)
    near = [(dy, step) for dy in (1, 0) for step in (2, 1, 3, 0)][:-1]
    fourth = []
    for dy, step in near:
        device = 64 * lax.rem(y + dy, 2) + 2 * (4 * ring + lax.rem(spot + step, 4)) + core
        fourth.append(remote(rows_of(group), rows_of(group), s4_send, s4_got, 4 * dy + step, (device, shard)))
        fourth[-1].start()
    sibling = at(0, 0, 1)[0]
    fifth = [remote(rows_of(group), rows_of(group), s5_send, s5_got, 0, (sibling, shard))]
    fifth[0].start()

    def to_owner(index):
        return pltpu.make_async_remote_copy(
            src_ref=moment_send.at[index], dst_ref=moment_got, send_sem=m_send.at[index], recv_sem=m_got,
            device_id=(8 * group + index, shard), device_id_type=MESH,
        )

    owner = rep != 64 * y

    @pl.when(hub)
    def _():
        for index in (2, 3, 7, 4, 5, 6):
            to_ring(index).start()
        for index in range(1, 8):
            to_owner(index).start()

        @pl.when(owner)
        def _():
            to_owner(0).start()

        @pl.when(jnp.logical_not(owner))
        def _():
            moment_got[...] = moment_send[0]

    for copy in ring3:
        copy.wait_recv()
    across_left, across_right = 2 * lax.rem(x + 3, 4) + 1 - y_hi, 2 * lax.rem(x + 1, 4) + 1 - y_hi
    ring4 = forward(across_left, across_right, 7)
    for copy in ring4:
        copy.start()
    total = total + product(across_left) + product(across_right)

    for (dy, step), copy in reversed(list(zip(near, fourth))):
        copy.wait_recv()
        number = 8 * lax.rem(y + dy, 2) + 2 * lax.rem(spot - step + 4, 4) + core
        fifth.append(remote(
            rows_of(number), rows_of(number), s5_send, s5_got, 4 * dy + step, (sibling, shard),
        ))
        fifth[-1].start()
    for copy in ring4:
        copy.wait_recv()
    total = total + product(2 * lax.rem(x + 2, 4) + 1 - y_hi)
    queries[...] = total.astype(jnp.bfloat16)
    for copy in fifth:
        copy.wait_recv()
    residual[...] = gathered[...]

    @pl.when(owner)
    def _():
        to_owner(0).wait_recv()

    new_momentum[...] = moment_got[...] + (decay_rate - slot_share) * slot

    for copy in first + ring1 + [across_copy] + ring2 + ring3 + fourth + ring4 + fifth:
        copy.wait_send()

    @pl.when(jnp.logical_not(hub))
    def _():
        to_hub(ring).wait_send()

    @pl.when(hub)
    def _():
        for index in range(1, 8):
            to_ring(index).wait_send()
            to_owner(index).wait_send()

        @pl.when(owner)
        def _():
            to_owner(0).wait_send()


def local(
    tokens, query_weight, global_params, local_params, momentum, inner_steps, replica_tokens, plan
):
    hbm = pl.BlockSpec(memory_space=pl.ANY)
    vmem = pl.BlockSpec(memory_space=pltpu.VMEM)
    smem = pl.BlockSpec(memory_space=pltpu.SMEM)
    dma = pltpu.SemaphoreType.DMA
    f32, bf16 = jnp.float32, jnp.bfloat16
    queries, residual, new_momentum = pl.pallas_call(
        kernel,
        out_shape=(
            jax.ShapeDtypeStruct((224, 128), bf16),
            jax.ShapeDtypeStruct((ROWS, COLS), bf16),
            jax.ShapeDtypeStruct((OWN, COLS), f32),
        ),
        in_specs=[hbm] * 7 + [smem],
        out_specs=(vmem, vmem, vmem),
        scratch_shapes=[
            pltpu.VMEM((224, 6144), bf16),
            pltpu.VMEM((8, ROWS, 128), bf16),
            pltpu.VMEM((ROWS, COLS), f32),
            pltpu.VMEM((ROWS, COLS), bf16),
            pltpu.VMEM((OWN, 8, COLS), f32),
            pltpu.VMEM((COLS, COLS), bf16),
            pltpu.VMEM((ROWS, COLS), bf16),
            pltpu.VMEM((1, 128), jnp.int32),
            pltpu.VMEM((1, 128), jnp.int32),
            pltpu.VMEM((16, GROUP, COLS), bf16),
            pltpu.VMEM((GROUP, COLS), f32),
            pltpu.VMEM((8, GROUP, COLS), f32),
            pltpu.VMEM((8, OWN, COLS), f32),
            pltpu.VMEM((OWN, COLS), f32),
            pltpu.VMEM((ROWS, COLS), bf16),
            dma((7,)),
            dma((16,)), dma((16,)),
            dma((8,)), dma((8,)),
            dma((8,)), dma((8,)),
            dma((8,)), dma((8,)),
            dma((8,)), dma((8,)),
            dma((9,)), dma((9,)),
            dma((8,)), dma(()),
        ],
        compiler_params=pltpu.CompilerParams(
            collective_id=0, has_side_effects=True, vmem_limit_bytes=60 * 1024 * 1024
        ),
        name="outer_step",
    )(
        tokens, query_weight, global_params, local_params, momentum.transpose(1, 0, 2),
        inner_steps.reshape(1, 128), replica_tokens.reshape(1, 128), plan,
    )
    new_params = keep * global_params + residual.astype(f32)
    return queries, new_params, new_momentum


def solution(mesh):
    return jax.shard_map(
        local,
        mesh=mesh,
        in_specs=(
            P(("rep", "fsdp"), None),
            P("rep", "fsdp", None),
            P("fsdp", None),
            P("rep", "fsdp", None),
            P(None, ("fsdp", "rep"), None),
            P(),
            P(),
            P(),
        ),
        out_specs=(P(("rep", "fsdp"), None), P("fsdp", None), P(("fsdp", "rep"), None)),
        check_vma=False,
    )
```

```python
import math

import jax
import jax.numpy as jnp
from jax import lax
from jax.experimental import pallas as pl
from jax.experimental.pallas import tpu as pltpu
from jax.sharding import PartitionSpec as P

BLOCK = 128
ROWS = 768
COLS = 256
GROUP = 48
LEVELS = 32767.0
OWN = 6
HALF = ROWS // 2
MESH = pl.DeviceIdType.MESH

decay_rate = 0.9
outer_rate = 0.7
keep = 1.0 - outer_rate * (1.0 + decay_rate)
slot_share = decay_rate * decay_rate / (1.0 + decay_rate)
root = 1.0 / math.sqrt(BLOCK)


def split3(values):
    high = values.astype(jnp.bfloat16)
    rest = values - high.astype(jnp.float32)
    middle = rest.astype(jnp.bfloat16)
    low = (rest - middle.astype(jnp.float32)).astype(jnp.bfloat16)
    return high, middle, low


def rotate(values, table):
    parts = [jnp.dot(part, table, preferred_element_type=jnp.float32) for part in split3(values)]
    return (parts[0] + parts[1] + parts[2]) * root


def kernel(
    tokens, query_weight, global_params, local_params, momentum, inner_steps, replica_tokens, plan,
    queries, residual, new_momentum,
    token_buf, weight_buf, global_buf, local_buf, momentum_buf, table_buf, term_buf, steps_buf, trained_buf,
    got1, own_sum, far_send, far_got, step_send, step_got, moment_send, moment_got, gathered,
    load_sem, s1_send, s1_got, s2_send, s2_got, s3_send, s3_got, s4_send, s4_got, s5_send, s5_got,
    w_send, w_got, m_send, m_got,
):
    rep, shard = lax.axis_index("rep"), lax.axis_index("fsdp")
    core = lax.rem(rep, 2)
    z = lax.rem(rep // 2, 32)
    y = rep // 64
    ring = z // 4
    kind = lax.rem(rep, 8)
    group = 8 * y + kind
    hub = ring == 0
    chunk = 8 * y + ring
    x, y_hi = shard // 2, lax.rem(shard, 2)
    sign = 1 - 2 * lax.rem(z, 2)

    def at(dy, dz, dc):
        ny, nz, nc = lax.rem(y + dy, 2), lax.rem(z + dz + 32, 32), lax.rem(core + dc, 2)
        return 64 * ny + 2 * nz + nc, 8 * ny + 2 * lax.rem(nz, 4) + nc

    right, left = 2 * lax.rem(x + 1, 4) + y_hi, 2 * lax.rem(x + 3, 4) + y_hi
    across = 2 * x + 1 - y_hi

    loads = []
    for index, (source, target) in enumerate((
        (local_params.at[0], local_buf), (global_params, global_buf), (momentum, momentum_buf),
        (query_weight.at[0], weight_buf.at[shard]), (tokens, token_buf),
        (inner_steps, steps_buf), (replica_tokens, trained_buf),
    )):
        loads.append(pltpu.make_async_copy(source, target, load_sem.at[index]))
        loads[-1].start()

    barrier = pltpu.get_barrier_semaphore()
    count = 0
    for dy in (0, 1):
        for dz in (0, 1, -1, 2, -2):
            for dc in (0, 1):
                if (dy, dz, dc) != (0, 0, 0):
                    pl.semaphore_signal(barrier, inc=1, device_id=(at(dy, dz, dc)[0], shard), device_id_type=MESH)
                    count += 1
    for other in (right, left, across):
        pl.semaphore_signal(barrier, inc=1, device_id=(rep, other), device_id_type=MESH)
        count += 1

    @pl.when(hub)
    def _():
        for step in range(1, 8):
            pl.semaphore_signal(barrier, inc=1, device_id=(64 * y + 8 * step + kind, shard), device_id_type=MESH)

    row = lax.broadcasted_iota(jnp.int32, (BLOCK, BLOCK), 0)
    col = lax.broadcasted_iota(jnp.int32, (BLOCK, BLOCK), 1)
    bits = row & col
    bits = bits ^ (bits >> 4)
    bits = bits ^ (bits >> 2)
    bits = bits ^ (bits >> 1)
    signs = (1 - 2 * (bits & 1)).astype(jnp.float32).astype(jnp.bfloat16)
    table_buf[...] = jnp.zeros_like(table_buf)
    table_buf[:BLOCK, :BLOCK] = signs
    table_buf[BLOCK:, BLOCK:] = signs

    loads[5].wait()
    loads[6].wait()
    ratio = trained_buf[...].astype(jnp.float32) / steps_buf[...].astype(jnp.float32)
    lane = lax.broadcasted_iota(jnp.int32, (1, 128), 1)
    mine = jnp.sum(jnp.where(lane == rep, ratio, 0.0), axis=1, keepdims=True)
    share = mine / jnp.sum(ratio, axis=1, keepdims=True)

    loads[0].wait()
    loads[1].wait()

    def code_rows(step, carry):
        rows = pl.ds(pl.multiple_of(step * 192, 192), 192)
        delta = global_buf[rows, :] - local_buf[rows, :].astype(jnp.float32)
        rotated = rotate(delta, table_buf[...])
        for side in (0, 1):
            block = rotated[:, side * BLOCK:(side + 1) * BLOCK]
            scale = jnp.max(jnp.abs(block), axis=1, keepdims=True) + 1e-06
            code = (block / scale).astype(jnp.bfloat16)
            term = code.astype(jnp.float32) * scale * share
            term_buf[rows, side * BLOCK:(side + 1) * BLOCK] = term.astype(jnp.bfloat16)
        return carry

    lax.fori_loop(0, ROWS // 192, code_rows, 0)

    loads[2].wait()
    fragment = lax.broadcasted_iota(jnp.int32, momentum_buf.shape, 1)
    slot = jnp.sum(jnp.where(fragment == plan[0], momentum_buf[...], 0.0), axis=1)
    spread = jnp.concatenate([jnp.where(kind == index, slot, 0.0) for index in range(8)], axis=0)
    chunk_rows = pl.ds(pl.multiple_of(chunk * GROUP, GROUP), GROUP)
    shifted = term_buf[chunk_rows, :].astype(jnp.float32) + slot_share * rotate(spread, table_buf[...])
    term_buf[chunk_rows, :] = shifted.astype(jnp.bfloat16)

    pl.semaphore_wait(barrier, count + jnp.where(hub, 0, 1))

    def remote(source, target, sends, gots, index, device):
        return pltpu.make_async_remote_copy(
            src_ref=source, dst_ref=target, send_sem=sends.at[index], recv_sem=gots.at[index],
            device_id=device, device_id_type=MESH,
        )

    hops = (0, 1, -1, 2 * sign)
    window = [(dy, index, dc) for dy in (1, 0) for index in (3, 1, 2, 0) for dc in (1, 0)][:-1]
    first = []
    for dy, index, dc in window:
        device, rows = at(dy, hops[index], dc)
        place = 8 * dy + 2 * index + dc
        first.append(remote(
            term_buf.at[pl.ds(pl.multiple_of(rows * GROUP, GROUP), GROUP), :], got1.at[place],
            s1_send, s1_got, place, (device, shard),
        ))
        first[-1].start()

    own_weight = query_weight.at[0]
    ring1 = [
        remote(own_weight, weight_buf.at[shard], w_send, w_got, 0, (rep, right)),
        remote(own_weight, weight_buf.at[shard], w_send, w_got, 1, (rep, left)),
    ]
    for copy in ring1:
        copy.start()

    loads[3].wait()
    loads[4].wait()

    def product(block):
        depth = pl.ds(pl.multiple_of(block * ROWS, ROWS), ROWS)
        return jnp.dot(token_buf[:, depth], weight_buf[block], preferred_element_type=jnp.float32)

    total = product(shard)

    summed = term_buf[pl.ds(pl.multiple_of(group * GROUP, GROUP), GROUP), :].astype(jnp.float32)
    for (dy, index, dc), copy in reversed(list(zip(window, first))):
        copy.wait_recv()
        summed = summed + got1[8 * dy + 2 * index + dc].astype(jnp.float32)
    own_sum[...] = summed
    peak = jnp.max(jnp.max(jnp.abs(summed), axis=1, keepdims=True), axis=0, keepdims=True)
    peak = jnp.maximum(peak, 1e-30)
    far_send[...] = jnp.round(summed * (LEVELS / peak)).astype(jnp.int32).astype(jnp.int16)
    step_send[...] = jnp.broadcast_to(peak * (1.0 / LEVELS), step_send.shape)

    def to_hub(index):
        return remote(far_send, far_got.at[index], s2_send, s2_got, index, (64 * y + kind, shard))

    def step_to_hub(index):
        return remote(step_send, step_got.at[index], s2_send, s2_got, index + 8, (64 * y + kind, shard))

    @pl.when(jnp.logical_not(hub))
    def _():
        step_to_hub(ring).start()
        to_hub(ring).start()

    across_copy = remote(own_weight, weight_buf.at[shard], w_send, w_got, 4, (rep, across))
    across_copy.start()

    block_left, block_right = left, right

    def forward(block_from_left, block_from_right, base):
        top, bottom = pl.ds(0, HALF), pl.ds(HALF, HALF)
        return [
            remote(weight_buf.at[block_from_left, top, :], weight_buf.at[block_from_left, top, :],
                   w_send, w_got, base, (rep, right)),
            remote(weight_buf.at[block_from_right, bottom, :], weight_buf.at[block_from_right, bottom, :],
                   w_send, w_got, base + 1, (rep, left)),
        ]

    for copy in ring1:
        copy.wait_recv()
    ring2 = forward(block_left, block_right, 2)
    for copy in ring2:
        copy.start()
    total = total + product(left) + product(right)

    across_copy.wait_recv()
    ring3 = [
        remote(weight_buf.at[across], weight_buf.at[across], w_send, w_got, 5, (rep, right)),
        remote(weight_buf.at[across], weight_buf.at[across], w_send, w_got, 6, (rep, left)),
    ]
    for copy in ring3:
        copy.start()
    far = 2 * lax.rem(x + 2, 4) + y_hi
    for copy in ring2:
        copy.wait_recv()
    total = total + product(across) + product(far)

    def rows_of(number):
        return gathered.at[pl.ds(pl.multiple_of(number * GROUP, GROUP), GROUP), :]

    def to_ring(index):
        return remote(rows_of(group), rows_of(group), s3_send, s3_got, index, (64 * y + 8 * index + kind, shard))

    @pl.when(hub)
    def _():
        summed = own_sum[...]
        for index in (1, 2, 3, 7, 6, 5, 4):
            step_to_hub(index).wait_recv()
            to_hub(index).wait_recv()
            summed = summed + far_got[index].astype(jnp.int32).astype(jnp.float32) * step_got[index, :1, :1]
        average = rotate(summed, table_buf[...])
        for index in range(8):
            moment_send[index] = average[OWN * index:OWN * (index + 1), :]
        own_global = global_buf[pl.ds(pl.multiple_of(group * GROUP, GROUP), GROUP), :]
        rest = (1.0 - keep) * (own_global - average)
        gathered[pl.ds(pl.multiple_of(group * GROUP, GROUP), GROUP), :] = rest.astype(jnp.bfloat16)
        for index in (1, 7, 4):
            to_ring(index).start()

    after = jnp.where(ring < 4, ring + 1, ring - 1)
    passes = jnp.logical_and(ring != 0, jnp.logical_and(ring != 3, jnp.logical_and(ring != 4, ring != 5)))

    @pl.when(jnp.logical_not(hub))
    def _():
        to_ring(ring).wait_recv()

    @pl.when(passes)
    def _():
        to_ring(after).start()

    spot = lax.rem(z, 4)
    near = [(dy, step) for dy in (1, 0) for step in (2, 1, 3, 0)][:-1]
    fourth = []
    for dy, step in near:
        device = 64 * lax.rem(y + dy, 2) + 2 * (4 * ring + lax.rem(spot + step, 4)) + core
        fourth.append(remote(rows_of(group), rows_of(group), s4_send, s4_got, 4 * dy + step, (device, shard)))
        fourth[-1].start()
    sibling = at(0, 0, 1)[0]
    fifth = [remote(rows_of(group), rows_of(group), s5_send, s5_got, 0, (sibling, shard))]
    fifth[0].start()

    def to_owner(index):
        return pltpu.make_async_remote_copy(
            src_ref=moment_send.at[index], dst_ref=moment_got, send_sem=m_send.at[index], recv_sem=m_got,
            device_id=(8 * group + index, shard), device_id_type=MESH,
        )

    owner = rep != 64 * y

    @pl.when(hub)
    def _():
        for index in range(1, 8):
            to_owner(index).start()

        @pl.when(owner)
        def _():
            to_owner(0).start()

        @pl.when(jnp.logical_not(owner))
        def _():
            moment_got[...] = moment_send[0]

    for copy in ring3:
        copy.wait_recv()
    across_left, across_right = 2 * lax.rem(x + 3, 4) + 1 - y_hi, 2 * lax.rem(x + 1, 4) + 1 - y_hi
    ring4 = forward(across_left, across_right, 7)
    for copy in ring4:
        copy.start()
    total = total + product(across_left) + product(across_right)

    for (dy, step), copy in reversed(list(zip(near, fourth))):
        copy.wait_recv()
        number = 8 * lax.rem(y + dy, 2) + 2 * lax.rem(spot - step + 4, 4) + core
        fifth.append(remote(
            rows_of(number), rows_of(number), s5_send, s5_got, 4 * dy + step, (sibling, shard),
        ))
        fifth[-1].start()
    for copy in ring4:
        copy.wait_recv()
    total = total + product(2 * lax.rem(x + 2, 4) + 1 - y_hi)
    queries[...] = total.astype(jnp.bfloat16)
    for copy in fifth:
        copy.wait_recv()
    residual[...] = gathered[...]

    @pl.when(owner)
    def _():
        to_owner(0).wait_recv()

    new_momentum[...] = moment_got[...] + (decay_rate - slot_share) * slot

    for copy in first + ring1 + [across_copy] + ring2 + ring3 + fourth + ring4 + fifth:
        copy.wait_send()

    @pl.when(jnp.logical_not(hub))
    def _():
        to_hub(ring).wait_send()
        step_to_hub(ring).wait_send()

    @pl.when(passes)
    def _():
        to_ring(after).wait_send()

    @pl.when(hub)
    def _():
        for index in (1, 7, 4):
            to_ring(index).wait_send()
        for index in range(1, 8):
            to_owner(index).wait_send()

        @pl.when(owner)
        def _():
            to_owner(0).wait_send()


def local(
    tokens, query_weight, global_params, local_params, momentum, inner_steps, replica_tokens, plan
):
    hbm = pl.BlockSpec(memory_space=pl.ANY)
    vmem = pl.BlockSpec(memory_space=pltpu.VMEM)
    smem = pl.BlockSpec(memory_space=pltpu.SMEM)
    dma = pltpu.SemaphoreType.DMA
    f32, bf16 = jnp.float32, jnp.bfloat16
    queries, residual, new_momentum = pl.pallas_call(
        kernel,
        out_shape=(
            pltpu.VMEM((224, 128), bf16),
            pltpu.VMEM((ROWS, COLS), bf16),
            pltpu.VMEM((OWN, COLS), f32),
        ),
        in_specs=[hbm] * 7 + [smem],
        out_specs=(vmem, vmem, vmem),
        scratch_shapes=[
            pltpu.VMEM((224, 6144), bf16),
            pltpu.VMEM((8, ROWS, 128), bf16),
            pltpu.VMEM((ROWS, COLS), f32),
            pltpu.VMEM((ROWS, COLS), bf16),
            pltpu.VMEM((OWN, 8, COLS), f32),
            pltpu.VMEM((COLS, COLS), bf16),
            pltpu.VMEM((ROWS, COLS), bf16),
            pltpu.VMEM((1, 128), jnp.int32),
            pltpu.VMEM((1, 128), jnp.int32),
            pltpu.VMEM((16, GROUP, COLS), bf16),
            pltpu.VMEM((GROUP, COLS), f32),
            pltpu.VMEM((GROUP, COLS), jnp.int16),
            pltpu.VMEM((8, GROUP, COLS), jnp.int16),
            pltpu.VMEM((8, BLOCK), f32),
            pltpu.VMEM((8, 8, BLOCK), f32),
            pltpu.VMEM((8, OWN, COLS), f32),
            pltpu.VMEM((OWN, COLS), f32),
            pltpu.VMEM((ROWS, COLS), bf16),
            dma((7,)),
            dma((16,)), dma((16,)),
            dma((16,)), dma((16,)),
            dma((8,)), dma((8,)),
            dma((8,)), dma((8,)),
            dma((8,)), dma((8,)),
            dma((9,)), dma((9,)),
            dma((8,)), dma(()),
        ],
        compiler_params=pltpu.CompilerParams(
            collective_id=0, has_side_effects=True, vmem_limit_bytes=60 * 1024 * 1024
        ),
        name="outer_step",
    )(
        tokens, query_weight, global_params, local_params, momentum.transpose(1, 0, 2),
        inner_steps.reshape(1, 128), replica_tokens.reshape(1, 128), plan,
    )
    new_params = keep * global_params + residual.astype(f32)
    return queries, new_params, new_momentum


def solution(mesh):
    return jax.shard_map(
        local,
        mesh=mesh,
        in_specs=(
            P(("rep", "fsdp"), None),
            P("rep", "fsdp", None),
            P("fsdp", None),
            P("rep", "fsdp", None),
            P(None, ("fsdp", "rep"), None),
            P(),
            P(),
            P(),
        ),
        out_specs=(P(("rep", "fsdp"), None), P("fsdp", None), P(("fsdp", "rep"), None)),
        check_vma=False,
    )
```

```python
import math

import jax
import jax.numpy as jnp
from jax import lax
from jax.experimental import pallas as pl
from jax.experimental.pallas import tpu as pltpu
from jax.sharding import PartitionSpec as P

BLOCK = 128
ROWS = 768
COLS = 256
GROUP = 48
LEVELS = 32767.0
OWN = 6
HALF = ROWS // 2
MESH = pl.DeviceIdType.MESH

decay_rate = 0.9
outer_rate = 0.7
keep = 1.0 - outer_rate * (1.0 + decay_rate)
slot_share = decay_rate * decay_rate / (1.0 + decay_rate)
root = 1.0 / math.sqrt(BLOCK)


def split3(values):
    high = values.astype(jnp.bfloat16)
    rest = values - high.astype(jnp.float32)
    middle = rest.astype(jnp.bfloat16)
    low = (rest - middle.astype(jnp.float32)).astype(jnp.bfloat16)
    return high, middle, low


def rotate(values, table):
    parts = [jnp.dot(part, table, preferred_element_type=jnp.float32) for part in split3(values)]
    return (parts[0] + parts[1] + parts[2]) * root


def kernel(
    tokens, query_weight, global_params, local_params, momentum, inner_steps, replica_tokens, plan,
    queries, residual, new_momentum,
    token_buf, weight_buf, global_buf, local_buf, momentum_buf, table_buf, term_buf, steps_buf, trained_buf, plan_buf,
    got1, own_sum, far_send, far_got, step_send, step_got, moment_send, moment_got, gathered,
    load_sem, s1_send, s1_got, s2_send, s2_got, s3_send, s3_got, s4_send, s4_got, s5_send, s5_got,
    w_send, w_got, m_send, m_got, told,
):
    rep, shard = lax.axis_index("rep"), lax.axis_index("fsdp")
    core = lax.rem(rep, 2)
    z = lax.rem(rep // 2, 32)
    y = rep // 64
    ring = z // 4
    kind = lax.rem(rep, 8)
    group = 8 * y + kind
    hub = ring == 0
    chunk = 8 * y + ring
    x, y_hi = shard // 2, lax.rem(shard, 2)
    sign = 1 - 2 * lax.rem(z, 2)

    def at(dy, dz, dc):
        ny, nz, nc = lax.rem(y + dy, 2), lax.rem(z + dz + 32, 32), lax.rem(core + dc, 2)
        return 64 * ny + 2 * nz + nc, 8 * ny + 2 * lax.rem(nz, 4) + nc

    right, left = 2 * lax.rem(x + 1, 4) + y_hi, 2 * lax.rem(x + 3, 4) + y_hi
    across = 2 * x + 1 - y_hi

    loads = []
    for index, (source, target) in enumerate((
        (local_params.at[0], local_buf), (global_params, global_buf), (momentum, momentum_buf),
        (query_weight.at[0], weight_buf.at[shard]), (tokens, token_buf),
        (inner_steps, steps_buf), (replica_tokens, trained_buf), (plan, plan_buf),
    )):
        loads.append(pltpu.make_async_copy(source, target, load_sem.at[index]))
        if index < 2:
            loads[-1].start()

    barrier = pltpu.get_barrier_semaphore()
    count = 0
    for dz in (2, -2, 1, -1, 0):
        for dy in (1, 0):
            for dc in (1, 0):
                if (dy, dz, dc) != (0, 0, 0):
                    pl.semaphore_signal(barrier, inc=1, device_id=(at(dy, dz, dc)[0], shard), device_id_type=MESH)
                    count += 1
    for other in (right, left, across):
        pl.semaphore_signal(barrier, inc=1, device_id=(rep, other), device_id_type=MESH)
        count += 1

    @pl.when(hub)
    def _():
        for step in (1, 2, 3, 5, 6, 7):
            pl.semaphore_signal(barrier, inc=1, device_id=(64 * y + 8 * step + kind, shard), device_id_type=MESH)

    @pl.when(ring == 4)
    def _():
        pl.semaphore_signal(barrier, inc=1, device_id=(64 * y + 8 * 3 + kind, shard), device_id_type=MESH)

    for index in (5, 6, 2, 7, 3, 4):
        loads[index].start()

    row = lax.broadcasted_iota(jnp.int32, (BLOCK, BLOCK), 0)
    col = lax.broadcasted_iota(jnp.int32, (BLOCK, BLOCK), 1)
    bits = row & col
    bits = bits ^ (bits >> 4)
    bits = bits ^ (bits >> 2)
    bits = bits ^ (bits >> 1)
    signs = (1 - 2 * (bits & 1)).astype(jnp.float32).astype(jnp.bfloat16)
    table_buf[...] = jnp.zeros_like(table_buf)
    table_buf[:BLOCK, :BLOCK] = signs
    table_buf[BLOCK:, BLOCK:] = signs

    loads[5].wait()
    loads[6].wait()
    ratio = trained_buf[...].astype(jnp.float32) / steps_buf[...].astype(jnp.float32)
    lane = lax.broadcasted_iota(jnp.int32, (1, 128), 1)
    mine = jnp.sum(jnp.where(lane == rep, ratio, 0.0), axis=1, keepdims=True)
    share = mine / jnp.sum(ratio, axis=1, keepdims=True)

    loads[0].wait()
    loads[1].wait()

    def code_rows(step, carry):
        rows = pl.ds(pl.multiple_of(step * 192, 192), 192)
        delta = global_buf[rows, :] - local_buf[rows, :].astype(jnp.float32)
        rotated = rotate(delta, table_buf[...])
        for side in (0, 1):
            block = rotated[:, side * BLOCK:(side + 1) * BLOCK]
            scale = jnp.max(jnp.abs(block), axis=1, keepdims=True) + 1e-06
            code = (block / scale).astype(jnp.bfloat16)
            term = code.astype(jnp.float32) * scale * share
            term_buf[rows, side * BLOCK:(side + 1) * BLOCK] = term.astype(jnp.bfloat16)
        return carry

    lax.fori_loop(0, ROWS // 192, code_rows, 0)

    loads[2].wait()
    loads[7].wait()
    chosen = jnp.broadcast_to(plan_buf[...], (OWN, COLS))
    slot = jnp.zeros((OWN, COLS), jnp.float32)
    for fragment in range(8):
        slot = slot + jnp.where(chosen == fragment, momentum_buf[:, fragment, :], 0.0)
    spread = jnp.concatenate([jnp.where(kind == index, slot, 0.0) for index in range(8)], axis=0)
    chunk_rows = pl.ds(pl.multiple_of(chunk * GROUP, GROUP), GROUP)
    shifted = term_buf[chunk_rows, :].astype(jnp.float32) + slot_share * rotate(spread, table_buf[...])
    term_buf[chunk_rows, :] = shifted.astype(jnp.bfloat16)

    from_hub = jnp.where(jnp.logical_or(hub, ring == 4), 0, 1)
    pl.semaphore_wait(barrier, count + from_hub + jnp.where(ring == 3, 1, 0))

    @pl.when(ring == 3)
    def _():
        pl.semaphore_signal(told, inc=1, device_id=(64 * y + 8 * 4 + kind, shard), device_id_type=MESH)

    def remote(source, target, sends, gots, index, device):
        return pltpu.make_async_remote_copy(
            src_ref=source, dst_ref=target, send_sem=sends.at[index], recv_sem=gots.at[index],
            device_id=device, device_id_type=MESH,
        )

    hops = (0, 1, -1, 2 * sign)
    window = [(dy, index, dc) for dy in (1, 0) for index in (3, 1, 2, 0) for dc in (1, 0)][:-1]
    first = []
    for dy, index, dc in window:
        device, rows = at(dy, hops[index], dc)
        place = 8 * dy + 2 * index + dc
        first.append(remote(
            term_buf.at[pl.ds(pl.multiple_of(rows * GROUP, GROUP), GROUP), :], got1.at[place],
            s1_send, s1_got, place, (device, shard),
        ))
        first[-1].start()

    own_weight = query_weight.at[0]
    ring1 = [
        remote(own_weight, weight_buf.at[shard], w_send, w_got, 0, (rep, right)),
        remote(own_weight, weight_buf.at[shard], w_send, w_got, 1, (rep, left)),
    ]
    for copy in ring1:
        copy.start()

    loads[3].wait()
    loads[4].wait()

    def product(block):
        depth = pl.ds(pl.multiple_of(block * ROWS, ROWS), ROWS)
        return jnp.dot(token_buf[:, depth], weight_buf[block], preferred_element_type=jnp.float32)

    total = product(shard)

    summed = term_buf[pl.ds(pl.multiple_of(group * GROUP, GROUP), GROUP), :].astype(jnp.float32)
    for (dy, index, dc), copy in reversed(list(zip(window, first))):
        copy.wait_recv()
        summed = summed + got1[8 * dy + 2 * index + dc].astype(jnp.float32)
    own_sum[...] = summed
    peak = jnp.max(jnp.max(jnp.abs(summed), axis=1, keepdims=True), axis=0, keepdims=True)
    peak = jnp.maximum(peak, 1e-30)
    far_send[...] = jnp.round(summed * (LEVELS / peak)).astype(jnp.int32).astype(jnp.int16)
    step_send[...] = jnp.broadcast_to(peak * (1.0 / LEVELS), step_send.shape)

    def to_hub(index):
        return remote(far_send, far_got.at[index], s2_send, s2_got, index, (64 * y + kind, shard))

    @pl.when(ring == 4)
    def _():
        pl.semaphore_wait(told, 1)

    def step_to_hub(index):
        return remote(step_send, step_got.at[index], s2_send, s2_got, index + 8, (64 * y + kind, shard))

    @pl.when(jnp.logical_not(hub))
    def _():
        step_to_hub(ring).start()
        to_hub(ring).start()

    across_copy = remote(own_weight, weight_buf.at[shard], w_send, w_got, 4, (rep, across))
    across_copy.start()

    block_left, block_right = left, right

    def forward(block_from_left, block_from_right, base):
        top, bottom = pl.ds(0, HALF), pl.ds(HALF, HALF)
        return [
            remote(weight_buf.at[block_from_left, top, :], weight_buf.at[block_from_left, top, :],
                   w_send, w_got, base, (rep, right)),
            remote(weight_buf.at[block_from_right, bottom, :], weight_buf.at[block_from_right, bottom, :],
                   w_send, w_got, base + 1, (rep, left)),
        ]

    for copy in ring1:
        copy.wait_recv()
    ring2 = forward(block_left, block_right, 2)
    for copy in ring2:
        copy.start()
    total = total + product(left) + product(right)

    across_copy.wait_recv()
    ring3 = [
        remote(weight_buf.at[across], weight_buf.at[across], w_send, w_got, 5, (rep, right)),
        remote(weight_buf.at[across], weight_buf.at[across], w_send, w_got, 6, (rep, left)),
    ]
    for copy in ring3:
        copy.start()
    far = 2 * lax.rem(x + 2, 4) + y_hi
    for copy in ring2:
        copy.wait_recv()
    total = total + product(across) + product(far)

    def rows_of(number):
        return gathered.at[pl.ds(pl.multiple_of(number * GROUP, GROUP), GROUP), :]

    def to_ring(index):
        return remote(rows_of(group), rows_of(group), s3_send, s3_got, index, (64 * y + 8 * index + kind, shard))

    @pl.when(hub)
    def _():
        summed = own_sum[...]
        for index in (1, 2, 3, 7, 6, 5, 4):
            step_to_hub(index).wait_recv()
            to_hub(index).wait_recv()
            summed = summed + far_got[index].astype(jnp.int32).astype(jnp.float32) * step_got[index, :1, :1]
        average = rotate(summed, table_buf[...])
        for index in range(8):
            moment_send[index] = average[OWN * index:OWN * (index + 1), :]
        own_global = global_buf[pl.ds(pl.multiple_of(group * GROUP, GROUP), GROUP), :]
        rest = (1.0 - keep) * (own_global - average)
        gathered[pl.ds(pl.multiple_of(group * GROUP, GROUP), GROUP), :] = rest.astype(jnp.bfloat16)
        for index in (1, 7, 4):
            to_ring(index).start()

    after = jnp.where(ring < 4, ring + 1, ring - 1)
    passes = jnp.logical_and(ring != 0, jnp.logical_and(ring != 3, jnp.logical_and(ring != 4, ring != 5)))

    @pl.when(jnp.logical_not(hub))
    def _():
        to_ring(ring).wait_recv()

    @pl.when(passes)
    def _():
        to_ring(after).start()

    spot = lax.rem(z, 4)
    near = [(dy, step) for dy in (1, 0) for step in (2, 1, 3, 0)][:-1]
    fourth = []
    for dy, step in near:
        device = 64 * lax.rem(y + dy, 2) + 2 * (4 * ring + lax.rem(spot + step, 4)) + core
        fourth.append(remote(rows_of(group), rows_of(group), s4_send, s4_got, 4 * dy + step, (device, shard)))
        fourth[-1].start()
    sibling = at(0, 0, 1)[0]
    fifth = [remote(rows_of(group), rows_of(group), s5_send, s5_got, 0, (sibling, shard))]
    fifth[0].start()

    def to_owner(index):
        return pltpu.make_async_remote_copy(
            src_ref=moment_send.at[index], dst_ref=moment_got, send_sem=m_send.at[index], recv_sem=m_got,
            device_id=(8 * group + index, shard), device_id_type=MESH,
        )

    owner = rep != 64 * y

    @pl.when(hub)
    def _():
        for index in range(1, 8):
            to_owner(index).start()

        @pl.when(owner)
        def _():
            to_owner(0).start()

        @pl.when(jnp.logical_not(owner))
        def _():
            moment_got[...] = moment_send[0]

    for copy in ring3:
        copy.wait_recv()
    across_left, across_right = 2 * lax.rem(x + 3, 4) + 1 - y_hi, 2 * lax.rem(x + 1, 4) + 1 - y_hi
    ring4 = forward(across_left, across_right, 7)
    for copy in ring4:
        copy.start()
    total = total + product(across_left) + product(across_right)

    for (dy, step), copy in reversed(list(zip(near, fourth))):
        copy.wait_recv()
        number = 8 * lax.rem(y + dy, 2) + 2 * lax.rem(spot - step + 4, 4) + core
        fifth.append(remote(
            rows_of(number), rows_of(number), s5_send, s5_got, 4 * dy + step, (sibling, shard),
        ))
        fifth[-1].start()
    for copy in ring4:
        copy.wait_recv()
    total = total + product(2 * lax.rem(x + 2, 4) + 1 - y_hi)
    queries[...] = total.astype(jnp.bfloat16)
    for copy in fifth:
        copy.wait_recv()
    residual[...] = gathered[...]

    @pl.when(owner)
    def _():
        to_owner(0).wait_recv()

    new_momentum[...] = moment_got[...] + (decay_rate - slot_share) * slot

    for copy in first + ring1 + [across_copy] + ring2 + ring3 + fourth + ring4 + fifth:
        copy.wait_send()

    @pl.when(jnp.logical_not(hub))
    def _():
        to_hub(ring).wait_send()
        step_to_hub(ring).wait_send()

    @pl.when(passes)
    def _():
        to_ring(after).wait_send()

    @pl.when(hub)
    def _():
        for index in (1, 7, 4):
            to_ring(index).wait_send()
        for index in range(1, 8):
            to_owner(index).wait_send()

        @pl.when(owner)
        def _():
            to_owner(0).wait_send()


def local(
    tokens, query_weight, global_params, local_params, momentum, inner_steps, replica_tokens, plan
):
    hbm = pl.BlockSpec(memory_space=pl.ANY)
    vmem = pl.BlockSpec(memory_space=pltpu.VMEM)
    dma = pltpu.SemaphoreType.DMA
    f32, bf16 = jnp.float32, jnp.bfloat16
    queries, residual, new_momentum = pl.pallas_call(
        kernel,
        out_shape=(
            pltpu.VMEM((224, 128), bf16),
            pltpu.VMEM((ROWS, COLS), bf16),
            pltpu.VMEM((OWN, COLS), f32),
        ),
        in_specs=[hbm] * 8,
        out_specs=(vmem, vmem, vmem),
        scratch_shapes=[
            pltpu.VMEM((224, 6144), bf16),
            pltpu.VMEM((8, ROWS, 128), bf16),
            pltpu.VMEM((ROWS, COLS), f32),
            pltpu.VMEM((ROWS, COLS), bf16),
            pltpu.VMEM((OWN, 8, COLS), f32),
            pltpu.VMEM((COLS, COLS), bf16),
            pltpu.VMEM((ROWS, COLS), bf16),
            pltpu.VMEM((1, 128), jnp.int32),
            pltpu.VMEM((1, 128), jnp.int32),
            pltpu.VMEM((1, 1), jnp.int32),
            pltpu.VMEM((16, GROUP, COLS), bf16),
            pltpu.VMEM((GROUP, COLS), f32),
            pltpu.VMEM((GROUP, COLS), jnp.int16),
            pltpu.VMEM((8, GROUP, COLS), jnp.int16),
            pltpu.VMEM((8, BLOCK), f32),
            pltpu.VMEM((8, 8, BLOCK), f32),
            pltpu.VMEM((8, OWN, COLS), f32),
            pltpu.VMEM((OWN, COLS), f32),
            pltpu.VMEM((ROWS, COLS), bf16),
            dma((8,)),
            dma((16,)), dma((16,)),
            dma((16,)), dma((16,)),
            dma((8,)), dma((8,)),
            dma((8,)), dma((8,)),
            dma((8,)), dma((8,)),
            dma((9,)), dma((9,)),
            dma((8,)), dma(()),
            pltpu.SemaphoreType.REGULAR,
        ],
        compiler_params=pltpu.CompilerParams(
            collective_id=0, has_side_effects=True, vmem_limit_bytes=60 * 1024 * 1024
        ),
        name="outer_step",
    )(
        tokens, query_weight, global_params, local_params, momentum.transpose(1, 0, 2),
        inner_steps.reshape(1, 128), replica_tokens.reshape(1, 128), plan.reshape(1, 1),
    )
    new_params = keep * global_params + residual.astype(f32)
    return queries, new_params, new_momentum


def solution(mesh):
    return jax.shard_map(
        local,
        mesh=mesh,
        in_specs=(
            P(("rep", "fsdp"), None),
            P("rep", "fsdp", None),
            P("fsdp", None),
            P("rep", "fsdp", None),
            P(None, ("fsdp", "rep"), None),
            P(),
            P(),
            P(),
        ),
        out_specs=(P(("rep", "fsdp"), None), P("fsdp", None), P(("fsdp", "rep"), None)),
        check_vma=False,
    )
```
